32 devices in a mesh: seq: 4 (over y, core), fsdp: 8 (over z, x).
Axes of the slice: x: 2, y: 2, z: 4, core: 2. Of those that a mesh axis runs over, the one named last changes fastest.
Arguments:
- frames_in: bfloat16 [8, 1024, 768], P('fsdp', 'seq'), may hold values from -6 to 6
- norm1_gain: bfloat16 [2, 768], P(None, 'fsdp'), may hold values from 0.25 to 1.75
- norm1_bias: bfloat16 [2, 768], P(None, 'fsdp'), may hold values from -3 to 3
- qkv_weight: bfloat16 [2, 768, 2304], P(None, 'fsdp'), may hold values from -0.3125 to 0.3125
- qv_bias: bfloat16 [2, 2, 768], P(None, None, 'fsdp'), may hold values from -0.59765625 to 0.59765625
- out_weight: bfloat16 [2, 768, 768], P(None, 'fsdp'), may hold values from -0.21875 to 0.21875
- out_bias: bfloat16 [2, 768], P(None, 'fsdp'), may hold values from -3 to 3
- norm2_gain: bfloat16 [2, 768], P(None, 'fsdp'), may hold values from 0.25 to 1.75
- norm2_bias: bfloat16 [2, 768], P(None, 'fsdp'), may hold values from -3 to 3
- fc1_weight: bfloat16 [2, 768, 3072], P(None, 'fsdp'), may hold values from -0.21875 to 0.21875
- fc1_bias: bfloat16 [2, 3072], P(None, 'fsdp'), may hold values from -3 to 3
- fc2_weight: bfloat16 [2, 3072, 768], P(None, 'fsdp'), may hold values from -0.109375 to 0.109375
- fc2_bias: bfloat16 [2, 768], P(None, 'fsdp'), may hold values from -3 to 3
- out_cotangent: bfloat16 [8, 1024, 768], P('fsdp', 'seq'), may hold values from -6 to 6
Outputs:
- frames_out: bfloat16 [8, 1024, 768], P('fsdp', 'seq')
- frames_grad: float32 [8, 1024, 768], P('fsdp', 'seq')
- norm1_gain_grad: float32 [2, 768], P(None, 'fsdp')
- norm1_bias_grad: float32 [2, 768], P(None, 'fsdp')
- qkv_weight_grad: float32 [2, 768, 2304], P(None, 'fsdp')
- qv_bias_grad: float32 [2, 2, 768], P(None, None, 'fsdp')
- out_weight_grad: float32 [2, 768, 768], P(None, 'fsdp')
- out_bias_grad: float32 [2, 768], P(None, 'fsdp')
- norm2_gain_grad: float32 [2, 768], P(None, 'fsdp')
- norm2_bias_grad: float32 [2, 768], P(None, 'fsdp')
- fc1_weight_grad: float32 [2, 768, 3072], P(None, 'fsdp')
- fc1_bias_grad: float32 [2, 3072], P(None, 'fsdp')
- fc2_weight_grad: float32 [2, 3072, 768], P(None, 'fsdp')
- fc2_bias_grad: float32 [2, 768], P(None, 'fsdp')
The draws below stay inside these ranges and needn't reach their ends.
All inputs are finite; a program needn't handle non-finite values.
Results may differ from the reference program's by a relative error of at most 0.023.
Values may be sent and summed in bfloat16 or wider, within the bound.
A program may use at most 192 MiB of HBM per device.

```python
import math
import jax
import jax.numpy as jnp
from jax import lax

D = 768
HEADS = 12
HEAD_DIM = 64
FF = 3072
LAYERS = 2
FRAMES = 1024
CLIPS = 8


def block_levels(stream_key, extent, cuts, smallest, high):
    level = 1.0
    for dim, blocks in cuts:
        heights = jax.random.uniform(jax.random.fold_in(jax.random.fold_in(stream_key, 6), dim), (blocks,), jnp.float32, smallest / len(cuts), high / len(cuts))
        level = level * jnp.repeat(jnp.exp(heights), extent[dim] // blocks).reshape((-1,) + (1,) * (len(extent) - 1 - dim))
    return level


def normal_values(stream_key, extent, scale, reach, pieces=(), dtype=jnp.bfloat16):
    values = jax.random.normal(stream_key, extent, jnp.float32) * scale
    if len(pieces) > 0:
        values = block_levels(stream_key, extent, pieces, -0.22, 0.18) * values
    return jnp.clip(values, min=-reach, max=reach).astype(dtype)


def setup_inputs(seed: int = 0) -> dict:
    splits = jax.random.split(jax.random.key(seed), 15)
    return {
        "frames_in": normal_values(splits[0], (CLIPS, FRAMES, D), 1.0, 6.0, ((0, 8), (1, 4))),
        "norm1_gain": jnp.clip(1.0 + 0.15 * jax.random.normal(splits[1], (LAYERS, D), jnp.float32), 0.25, 1.75).astype(jnp.bfloat16),
        "norm1_bias": normal_values(splits[2], (LAYERS, D), 0.5, 3.0, ((1, 8),)),
        "qkv_weight": normal_values(splits[3], (LAYERS, D, 3 * D), (D // 2) ** -0.5, 0.3125, ((1, 8),)),
        "qv_bias": normal_values(splits[4], (LAYERS, 2, D), 0.1, 0.59765625, ((2, 8),)),
        "out_weight": normal_values(splits[5], (LAYERS, D, D), D ** -0.5, 0.21875, ((1, 8),)),
        "out_bias": normal_values(splits[6], (LAYERS, D), 0.5, 3.0, ((1, 8),)),
        "norm2_gain": jnp.clip(1.0 + 0.15 * jax.random.normal(splits[7], (LAYERS, D), jnp.float32), 0.25, 1.75).astype(jnp.bfloat16),
        "norm2_bias": normal_values(splits[8], (LAYERS, D), 0.5, 3.0, ((1, 8),)),
        "fc1_weight": normal_values(splits[9], (LAYERS, D, FF), D ** -0.5, 0.21875, ((1, 8),)),
        "fc1_bias": normal_values(splits[10], (LAYERS, FF), 0.5, 3.0, ((1, 8),)),
        "fc2_weight": normal_values(splits[11], (LAYERS, FF, D), FF ** -0.5, 0.109375, ((1, 8),)),
        "fc2_bias": normal_values(splits[12], (LAYERS, D), 0.5, 3.0, ((1, 8),)),
        "out_cotangent": normal_values(splits[13], (CLIPS, FRAMES, D), 1.0, 6.0, ((0, 8), (1, 4))),
    }


@jax.custom_vjp
def low(v):
    return lax.optimization_barrier(v.astype(jnp.bfloat16)).astype(jnp.float32)

@jax.custom_vjp
def low_back(v):
    return v

def low_keep(v):
    return (low(v), None)

def low_pass(kept, grad):
    return (grad,)

def back_keep(v):
    return (v, None)

def back_low(kept, grad):
    return (low(grad),)
low.defvjp(low_keep, low_pass)
low_back.defvjp(back_keep, back_low)
EPSILON = 1e-05
HIGHEST_PRECISION = lax.Precision.HIGHEST

def norm_rows(values, gain, shift):
    center = lax.optimization_barrier(jnp.mean(values, axis=-1, keepdims=True))
    centred = values - center
    spread = lax.optimization_barrier(jnp.mean(centred * centred, axis=-1, keepdims=True))
    return centred * lax.rsqrt(spread + EPSILON) * gain + shift

def qkv_shift(pair_bias):
    query_part = pair_bias[0].reshape(HEADS, 1, HEAD_DIM)
    value_part = pair_bias[1].reshape(HEADS, 1, HEAD_DIM)
    joined = jnp.concatenate([query_part, jnp.zeros_like(query_part), value_part], axis=1)
    return joined.reshape(3 * D)

def attend_clip(packed):
    parts = packed.reshape(FRAMES, HEADS, 3, HEAD_DIM)
    scale = HEAD_DIM ** (-0.5)
    scores = low_back(jnp.einsum('qhd,khd->hqk', parts[:, :, 0], parts[:, :, 1], precision=HIGHEST_PRECISION) * scale)
    weights = low(jax.nn.softmax(scores, axis=-1))
    mixed = jnp.einsum('hqk,khd->qhd', weights, parts[:, :, 2], precision=HIGHEST_PRECISION)
    return mixed.reshape(FRAMES, D)

def layer_apply(stream, params):
    gain_one, shift_one, w_qkv, qv_pair, w_out, out_shift, gain_two, shift_two, w_up, up_shift, w_down, down_shift = params
    normed_one = low(norm_rows(stream, gain_one, shift_one))
    projected = low_back(low(jnp.einsum('cfi,io->cfo', normed_one, w_qkv, precision=HIGHEST_PRECISION) + qkv_shift(qv_pair)))
    mixed = low_back(low(lax.map(jax.checkpoint(attend_clip), projected)))
    attended = stream + low_back(jnp.einsum('cfi,io->cfo', mixed, w_out, precision=HIGHEST_PRECISION) + out_shift)
    normed_two = low(norm_rows(attended, gain_two, shift_two))
    hidden = low_back(jnp.einsum('cfi,io->cfo', normed_two, w_up, precision=HIGHEST_PRECISION) + up_shift)
    activated = low(jax.nn.gelu(hidden, approximate=False))
    return attended + low_back(jnp.einsum('cfi,io->cfo', activated, w_down, precision=HIGHEST_PRECISION) + down_shift)

def forward_pass(stream, weights):
    for layer_index in range(LAYERS):
        stream = layer_apply(stream, tuple((piece[layer_index] for piece in weights)))
    return stream

def reference(frames_in, norm1_gain, norm1_bias, qkv_weight, qv_bias, out_weight, out_bias, norm2_gain, norm2_bias, fc1_weight, fc1_bias, fc2_weight, fc2_bias, out_cotangent):
    weights = tuple((piece.astype(jnp.float32) for piece in (norm1_gain, norm1_bias, qkv_weight, qv_bias, out_weight, out_bias, norm2_gain, norm2_bias, fc1_weight, fc1_bias, fc2_weight, fc2_bias)))
    group_size = math.gcd(CLIPS, max(1, 4096 // FRAMES))
    blocks = CLIPS // group_size
    inputs = frames_in.reshape(blocks, group_size, FRAMES, D)
    cotangent = out_cotangent.reshape(blocks, group_size, FRAMES, D)

    def scan_step(totals, block_pair):
        clip_block, upstream = block_pair
        result, pullback = jax.vjp(forward_pass, clip_block.astype(jnp.float32), weights)
        grad_frames, grad_weights = pullback(upstream.astype(jnp.float32))
        totals = jax.tree.map(jnp.add, totals, grad_weights)
        return (totals, (result.astype(jnp.bfloat16), grad_frames))
    initial = jax.tree.map(jnp.zeros_like, weights)
    totals, (outputs, grads) = lax.scan(scan_step, initial, (inputs, cotangent))
    return (outputs.reshape(CLIPS, FRAMES, D), grads.reshape(CLIPS, FRAMES, D), totals[0], totals[1], totals[2], totals[3], totals[4], totals[5], totals[6], totals[7], totals[8], totals[9], totals[10], totals[11])
```

```python
from functools import partial
import math

import jax
import jax.numpy as jnp
from jax import lax
from jax.sharding import PartitionSpec as P

D = 768
HEADS = 12
HEAD_DIM = 64


EPSILON = 1e-05


def norm_rows(values, gain, shift):
    center = jnp.mean(values, axis=-1, keepdims=True)
    centred = values - center
    spread = jnp.mean(centred * centred, axis=-1, keepdims=True)
    return centred * lax.rsqrt(spread + EPSILON) * gain + shift


def qkv_shift(pair_bias):
    query_part = pair_bias[0].reshape(HEADS, 1, HEAD_DIM)
    value_part = pair_bias[1].reshape(HEADS, 1, HEAD_DIM)
    joined = jnp.concatenate([query_part, jnp.zeros_like(query_part), value_part], axis=1)
    return joined.reshape(3 * D)


BF = jnp.bfloat16
F32 = jnp.float32


def seq_gather(block):
    return lax.all_gather(block, "seq", axis=1, tiled=True)


def seq_reduce(partial_sum):
    summed = lax.psum_scatter(partial_sum.astype(BF), "seq", scatter_dimension=1, tiled=True)
    return summed.astype(F32)


def dot_in(rows, matrix):
    return jnp.einsum("cfi,io->cfo", rows, matrix, preferred_element_type=F32)


def dot_back(rows, matrix):
    return jnp.einsum("cfo,io->cfi", rows, matrix, preferred_element_type=F32)


def dot_grad(left, right):
    return jnp.einsum("cfi,cfo->io", left, right, preferred_element_type=F32)


def take_part(array, axis, parts, index):
    size = array.shape[axis] // parts
    return lax.dynamic_slice_in_dim(array, index * size, size, axis)


def put_part(part, axis, parts, index):
    shape = list(part.shape)
    shape[axis] = shape[axis] * parts
    return lax.dynamic_update_slice_in_dim(
        jnp.zeros(shape, part.dtype), part, index * part.shape[axis], axis
    )


def layer_forward(stream, weights):
    gain_one, shift_one, w_qkv, qkv_add, w_out, out_shift, gain_two, shift_two, w_up, up_shift, w_down, down_shift = weights
    normed_one = seq_gather(norm_rows(stream, gain_one, shift_one).astype(BF))
    heads = (dot_in(normed_one, w_qkv) + qkv_add).astype(BF)
    outs = [attend_forward(heads[clip]) for clip in range(heads.shape[0])]
    mixed = jnp.stack([pair[0] for pair in outs])
    log_total = jnp.stack([pair[1] for pair in outs])
    attended = stream + (seq_reduce(dot_in(mixed, w_out)) + out_shift)
    normed_two = seq_gather(norm_rows(attended, gain_two, shift_two).astype(BF))
    hidden = dot_in(normed_two, w_up) + up_shift
    activated = jax.nn.gelu(hidden, approximate=False).astype(BF)
    result = attended + (seq_reduce(dot_in(activated, w_down)) + down_shift)
    return (stream, normed_one, heads, log_total, mixed, attended, normed_two, hidden, activated), result


def sum_rows(rows):
    return jnp.sum(rows.astype(F32), axis=(0, 1))


def layer_backward(upstream, weights, state, seq_index, seq_size, fsdp_size):
    gain_one, shift_one, w_qkv, qkv_add, w_out, out_shift, gain_two, shift_two, w_up, up_shift, w_down, down_shift = weights
    stream, normed_one, heads, log_total, mixed, attended, normed_two, hidden, activated = state
    grad_down_local = upstream.astype(BF)
    down_shift_grad = sum_rows(grad_down_local)
    grad_down = seq_gather(grad_down_local)
    w_down_grad = dot_grad(activated, grad_down)
    grad_active = dot_back(grad_down, w_down)
    gelu_pull = jax.vjp(partial(jax.nn.gelu, approximate=False), hidden)[1]
    grad_hidden = gelu_pull(grad_active)[0].astype(BF)
    up_shift_grad = sum_rows(grad_hidden)
    w_up_grad = dot_grad(normed_two, grad_hidden)
    grad_normed_two = seq_reduce(dot_back(grad_hidden, w_up))
    _, pull_two = jax.vjp(norm_rows, attended, gain_two, shift_two)
    grad_attended, gain_two_grad, shift_two_grad = pull_two(grad_normed_two)
    grad_attended = grad_attended + upstream
    grad_out_local = grad_attended.astype(BF)
    out_shift_grad = sum_rows(grad_out_local)
    grad_out = seq_gather(grad_out_local)
    w_out_grad = dot_grad(mixed, grad_out)
    grad_mixed = dot_back(grad_out, w_out).astype(BF)
    grad_projected = jnp.stack(
        [
            attend_backward((heads[clip], log_total[clip], grad_mixed[clip]))
            for clip in range(heads.shape[0])
        ]
    )
    qkv_add_grad = sum_rows(grad_projected)
    w_qkv_grad = dot_grad(normed_one, grad_projected)
    grad_normed_one = seq_reduce(dot_back(grad_projected, w_qkv))
    _, pull_one = jax.vjp(norm_rows, stream, gain_one, shift_one)
    grad_stream, gain_one_grad, shift_one_grad = pull_one(grad_normed_one)
    grad_stream = grad_stream + grad_attended

    out_columns = lax.all_to_all(w_out_grad.astype(BF), "seq", split_axis=1, concat_axis=0, tiled=True)
    big = jnp.concatenate(
        [w_up_grad.astype(BF), w_down_grad.astype(BF), w_qkv_grad.astype(BF), out_columns], axis=1
    )
    local_heads = qkv_add_grad.shape[0] // (3 * HEAD_DIM)
    triple = qkv_add_grad.reshape(local_heads, 3, HEAD_DIM)
    up_parts = put_part(up_shift_grad.reshape(fsdp_size, -1), 1, seq_size, seq_index)
    small = jnp.concatenate(
        [
            gain_one_grad,
            shift_one_grad,
            put_part(triple[:, 0].reshape(-1), 0, seq_size, seq_index),
            put_part(triple[:, 2].reshape(-1), 0, seq_size, seq_index),
            out_shift_grad,
            gain_two_grad,
            shift_two_grad,
            down_shift_grad,
            up_parts.reshape(-1),
        ]
    )
    return grad_stream, big, small


def reduce_big(big):
    owned = lax.psum_scatter(big, "fsdp", scatter_dimension=0, tiled=True)
    return lax.all_gather(owned, "seq", axis=0, tiled=False)


def unpack_big(gathered, sizes):
    up, down, qkv, out = sizes
    spots = [0, up, up + down, up + down + qkv, up + down + qkv + out]
    rows = gathered.shape[1]
    members = [gathered[:, :, spots[i] : spots[i + 1]].astype(F32) for i in range(4)]
    fsdp_size = D // rows
    seq_size = gathered.shape[0]
    w_up = members[0].reshape(seq_size, rows, fsdp_size, -1).transpose(1, 2, 0, 3).reshape(rows, -1)
    w_down = members[1].reshape(seq_size * rows, -1)
    w_qkv = members[2].transpose(1, 0, 2).reshape(rows, -1)
    w_out = members[3].transpose(1, 0, 2).reshape(rows, -1)
    return w_qkv, w_out, w_up, w_down


def attend_forward(packed):
    frames = packed.shape[0]
    local_heads = packed.shape[1] // (3 * HEAD_DIM)
    parts = packed.reshape(frames, local_heads, 3, HEAD_DIM)
    scores = jnp.einsum(
        "qhd,khd->hqk", parts[:, :, 0], parts[:, :, 1], preferred_element_type=jnp.float32
    ) * HEAD_DIM ** (-0.5)
    peak_score = jnp.max(scores, axis=-1, keepdims=True)
    expanded = jnp.exp(scores - peak_score)
    totals = jnp.sum(expanded, axis=-1, keepdims=True)
    weights = (expanded / totals).astype(jnp.bfloat16)
    mixed = jnp.einsum("hqk,khd->qhd", weights, parts[:, :, 2], preferred_element_type=jnp.float32)
    return (
        mixed.reshape(frames, local_heads * HEAD_DIM).astype(jnp.bfloat16),
        (peak_score + jnp.log(totals))[..., 0],
    )


def attend_backward(inputs):
    packed, log_total, incoming = inputs
    frames = packed.shape[0]
    local_heads = packed.shape[1] // (3 * HEAD_DIM)
    parts = packed.reshape(frames, local_heads, 3, HEAD_DIM)
    queries = parts[:, :, 0]
    keys_local = parts[:, :, 1]
    values_local = parts[:, :, 2]
    scale = HEAD_DIM ** (-0.5)
    scores = (
        jnp.einsum("qhd,khd->hqk", queries, keys_local, preferred_element_type=jnp.float32) * scale
    )
    probs = jnp.exp(scores - log_total[..., None])
    incoming_heads = incoming.reshape(frames, local_heads, HEAD_DIM)
    grad_probs = jnp.einsum(
        "qhd,khd->hqk", incoming_heads, values_local, preferred_element_type=jnp.float32
    )
    grad_values = jnp.einsum(
        "hqk,qhd->khd",
        probs.astype(jnp.bfloat16),
        incoming_heads,
        preferred_element_type=jnp.float32,
    )
    grad_scores = (
        probs * (grad_probs - jnp.sum(probs * grad_probs, axis=-1, keepdims=True))
    ).astype(jnp.bfloat16)
    grad_queries = (
        jnp.einsum("hqk,khd->qhd", grad_scores, keys_local, preferred_element_type=jnp.float32)
        * scale
    )
    grad_keys = (
        jnp.einsum("hqk,qhd->khd", grad_scores, queries, preferred_element_type=jnp.float32) * scale
    )
    stacked = jnp.stack([grad_queries, grad_keys, grad_values], axis=2)
    return stacked.reshape(frames, local_heads * 3 * HEAD_DIM).astype(jnp.bfloat16)


def local(
    frames_in,
    norm1_gain,
    norm1_bias,
    qkv_weight,
    qv_bias,
    out_weight,
    out_bias,
    norm2_gain,
    norm2_bias,
    fc1_weight,
    fc1_bias,
    fc2_weight,
    fc2_bias,
    out_cotangent,
):
    shards = (
        norm1_gain,
        norm1_bias,
        qkv_weight,
        qv_bias,
        out_weight,
        out_bias,
        norm2_gain,
        norm2_bias,
        fc1_weight,
        fc1_bias,
        fc2_weight,
        fc2_bias,
    )
    layer_count = qkv_weight.shape[0]
    fsdp_size = lax.axis_size("fsdp")
    seq_size = lax.axis_size("seq")
    seq_index = lax.axis_index("seq")
    owner = lax.axis_index("fsdp")
    rows = qkv_weight.shape[1]
    part_rows = fc1_bias.shape[1] // seq_size
    hidden_local = fsdp_size * part_rows

    small_in = jnp.concatenate(
        [norm1_gain, norm1_bias, qv_bias[:, 0], qv_bias[:, 1], out_bias, norm2_gain, norm2_bias, fc2_bias, fc1_bias],
        axis=1,
    )
    small_all = lax.all_gather(small_in.reshape(-1), "fsdp", axis=0, tiled=False)
    small_all = small_all.reshape(fsdp_size, layer_count, -1).astype(F32)

    weights = []
    for level in range(layer_count):
        up_part = take_part(fc1_weight[level].reshape(rows, fsdp_size, -1), 2, seq_size, seq_index)
        packed = jnp.concatenate(
            [
                up_part.reshape(rows, hidden_local),
                take_part(fc2_weight[level], 0, seq_size, seq_index),
                take_part(qkv_weight[level], 1, seq_size, seq_index),
                out_weight[level],
            ],
            axis=1,
        )
        packed = lax.all_gather(packed, "fsdp", axis=0, tiled=True)
        third = 3 * D // seq_size
        w_up = packed[:, :hidden_local]
        w_down = packed[:, hidden_local : hidden_local + D]
        w_qkv = packed[:, hidden_local + D : hidden_local + D + third]
        w_out = take_part(packed[:, hidden_local + D + third :], 0, seq_size, seq_index)
        pieces = small_all[:, level]
        vectors = [pieces[:, i * rows : (i + 1) * rows].reshape(D) for i in range(8)]
        gain_one, shift_one, query_add, value_add, out_shift, gain_two, shift_two, down_shift = vectors
        up_shift = take_part(pieces[:, 8 * rows :], 1, seq_size, seq_index).reshape(hidden_local)
        qkv_add = take_part(qkv_shift(jnp.stack([query_add, value_add])), 0, seq_size, seq_index)
        weights.append(
            (gain_one, shift_one, w_qkv, qkv_add, w_out, out_shift, gain_two, shift_two, w_up, up_shift, w_down, down_shift)
        )

    stream = frames_in.astype(F32)
    saved = []
    for level in range(layer_count):
        kept, stream = layer_forward(stream, weights[level])
        saved.append(kept)
    frames_out = stream.astype(BF)
    upstream = out_cotangent.astype(F32)
    reduced = [None] * layer_count
    smalls = [None] * layer_count
    for level in reversed(range(layer_count)):
        upstream, big, small = layer_backward(
            upstream, weights[level], saved[level], seq_index, seq_size, fsdp_size
        )
        smalls[level] = small
        reduced[level] = unpack_big(
            reduce_big(big), (hidden_local, D, 3 * D // seq_size, D // seq_size)
        )
    small_sum = lax.psum(jnp.stack(smalls), ("seq", "fsdp"))
    vectors = [take_part(small_sum[:, i * D : (i + 1) * D], 1, fsdp_size, owner) for i in range(8)]
    up_sum = take_part(small_sum[:, 8 * D :], 1, fsdp_size, owner)
    qkv_grad, out_grad, up_grad, down_grad = [
        jnp.stack([reduced[level][member] for level in range(layer_count)]) for member in range(4)
    ]
    return (
        frames_out,
        upstream,
        vectors[0],
        vectors[1],
        qkv_grad,
        jnp.stack([vectors[2], vectors[3]], axis=1),
        out_grad,
        vectors[4],
        vectors[5],
        vectors[6],
        up_grad,
        up_sum,
        down_grad,
        vectors[7],
    )


def solution(mesh):
    in_specs = (
        P("fsdp", "seq", None),
        P(None, "fsdp"),
        P(None, "fsdp"),
        P(None, "fsdp", None),
        P(None, None, "fsdp"),
        P(None, "fsdp", None),
        P(None, "fsdp"),
        P(None, "fsdp"),
        P(None, "fsdp"),
        P(None, "fsdp", None),
        P(None, "fsdp"),
        P(None, "fsdp", None),
        P(None, "fsdp"),
        P("fsdp", "seq", None),
    )
    out_specs = (
        P("fsdp", "seq", None),
        P("fsdp", "seq", None),
        P(None, "fsdp"),
        P(None, "fsdp"),
        P(None, "fsdp", None),
        P(None, None, "fsdp"),
        P(None, "fsdp", None),
        P(None, "fsdp"),
        P(None, "fsdp"),
        P(None, "fsdp"),
        P(None, "fsdp", None),
        P(None, "fsdp"),
        P(None, "fsdp", None),
        P(None, "fsdp"),
    )
    return jax.shard_map(local, mesh=mesh, in_specs=in_specs, out_specs=out_specs, check_vma=False)
```

```python
from functools import partial
import math

import jax
import jax.numpy as jnp
from jax import lax
from jax.experimental import pallas as pl
from jax.experimental.pallas import tpu as pltpu
from jax.sharding import PartitionSpec as P

D = 768
HEADS = 12
HEAD_DIM = 64


EPSILON = 1e-05


def norm_rows(values, gain, shift):
    center = jnp.mean(values, axis=-1, keepdims=True)
    centred = values - center
    spread = jnp.mean(centred * centred, axis=-1, keepdims=True)
    return centred * lax.rsqrt(spread + EPSILON) * gain + shift


def qkv_shift(pair_bias):
    query_part = pair_bias[0].reshape(HEADS, 1, HEAD_DIM)
    value_part = pair_bias[1].reshape(HEADS, 1, HEAD_DIM)
    joined = jnp.concatenate([query_part, jnp.zeros_like(query_part), value_part], axis=1)
    return joined.reshape(3 * D)


BF = jnp.bfloat16
F32 = jnp.float32


MESH_ID = pl.DeviceIdType.MESH


def partners():
    me = lax.axis_index("seq")
    core = me + 1 - 2 * lax.rem(me, 2)
    across = lax.rem(me + 2, 4)
    return me, core, across, lax.rem(core + 2, 4)


def greet(core, across):
    barrier = pltpu.get_barrier_semaphore()
    for other in (core, across):
        pl.semaphore_signal(barrier, inc=1, device_id={"seq": other}, device_id_type=MESH_ID)
    pl.semaphore_wait(barrier, 2)


def send(src, dst, send_sem, recv_sem, other):
    return pltpu.make_async_remote_copy(
        src_ref=src,
        dst_ref=dst,
        send_sem=send_sem,
        recv_sem=recv_sem,
        device_id={"seq": other},
        device_id_type=MESH_ID,
    )


def gather_kernel(block_ref, whole_ref, land, send_sem, recv_sem):
    me, core, across, far = partners()
    greet(core, across)
    over = send(block_ref, land.at[1], send_sem.at[1], recv_sem.at[1], across)
    over.start()
    beside = send(block_ref, land.at[0], send_sem.at[0], recv_sem.at[0], core)
    beside.start()
    whole_ref[me] = block_ref[...]
    over.wait_recv()
    relay = send(land.at[1], land.at[2], send_sem.at[2], recv_sem.at[2], core)
    relay.start()
    whole_ref[across] = land[1]
    beside.wait_recv()
    whole_ref[core] = land[0]
    relay.wait_recv()
    whole_ref[far] = land[2]
    over.wait_send()
    beside.wait_send()
    relay.wait_send()


def reduce_kernel(parts_ref, total_ref, land, pair, send_sem, recv_sem):
    me, core, across, far = partners()
    greet(core, across)
    first = send(parts_ref.at[far], land.at[0], send_sem.at[0], recv_sem.at[0], core)
    first.start()
    second = send(parts_ref.at[core], land.at[1], send_sem.at[1], recv_sem.at[1], core)
    second.start()
    first.wait_recv()
    pair[...] = (parts_ref[across].astype(F32) + land[0].astype(F32)).astype(BF)
    last = send(pair, land.at[2], send_sem.at[2], recv_sem.at[2], across)
    last.start()
    second.wait_recv()
    total_ref[...] = parts_ref[me].astype(F32) + land[1].astype(F32)
    last.wait_recv()
    total_ref[...] += land[2].astype(F32)
    first.wait_send()
    second.wait_send()
    last.wait_send()


def kernel_params(number):
    return pltpu.CompilerParams(
        collective_id=number, has_side_effects=True, vmem_limit_bytes=24 * 1024 * 1024
    )


def seq_gather(block):
    clips, frames, width = block.shape
    rows = clips * frames
    whole = pl.pallas_call(
        gather_kernel,
        out_shape=jax.ShapeDtypeStruct((4, rows, width), BF),
        in_specs=[pl.BlockSpec(memory_space=pltpu.VMEM)],
        out_specs=pl.BlockSpec(memory_space=pltpu.VMEM),
        scratch_shapes=[
            pltpu.VMEM((3, rows, width), BF),
            pltpu.SemaphoreType.DMA((3,)),
            pltpu.SemaphoreType.DMA((3,)),
        ],
        compiler_params=kernel_params(0),
        cost_estimate=pl.CostEstimate(flops=0, bytes_accessed=16 * rows * width, transcendentals=0),
    )(block.reshape(rows, width))
    whole = whole.reshape(4, clips, frames, width).swapaxes(0, 1)
    return whole.reshape(clips, 4 * frames, width)


def seq_reduce(partial_sum):
    clips, all_frames, width = partial_sum.shape
    frames = all_frames // 4
    rows = clips * frames
    parts = partial_sum.astype(BF).reshape(clips, 4, frames, width).swapaxes(0, 1)
    total = pl.pallas_call(
        reduce_kernel,
        out_shape=jax.ShapeDtypeStruct((rows, width), F32),
        in_specs=[pl.BlockSpec(memory_space=pltpu.VMEM)],
        out_specs=pl.BlockSpec(memory_space=pltpu.VMEM),
        scratch_shapes=[
            pltpu.VMEM((3, rows, width), BF),
            pltpu.VMEM((rows, width), BF),
            pltpu.SemaphoreType.DMA((3,)),
            pltpu.SemaphoreType.DMA((3,)),
        ],
        compiler_params=kernel_params(1),
        cost_estimate=pl.CostEstimate(flops=0, bytes_accessed=16 * rows * width, transcendentals=0),
    )(parts.reshape(4, rows, width))
    return total.reshape(clips, frames, width)


def dot_in(rows, matrix):
    return jnp.einsum("cfi,io->cfo", rows, matrix, preferred_element_type=F32)


def dot_back(rows, matrix):
    return jnp.einsum("cfo,io->cfi", rows, matrix, preferred_element_type=F32)


def dot_grad(left, right):
    return jnp.einsum("cfi,cfo->io", left, right, preferred_element_type=F32)


def take_part(array, axis, parts, index):
    size = array.shape[axis] // parts
    return lax.dynamic_slice_in_dim(array, index * size, size, axis)


def put_part(part, axis, parts, index):
    shape = list(part.shape)
    shape[axis] = shape[axis] * parts
    return lax.dynamic_update_slice_in_dim(
        jnp.zeros(shape, part.dtype), part, index * part.shape[axis], axis
    )


def layer_forward(stream, weights):
    gain_one, shift_one, w_qkv, qkv_add, w_out, out_shift, gain_two, shift_two, w_up, up_shift, w_down, down_shift = weights
    normed_one = seq_gather(norm_rows(stream, gain_one, shift_one).astype(BF))
    heads = (dot_in(normed_one, w_qkv) + qkv_add).astype(BF)
    outs = [attend_forward(heads[clip]) for clip in range(heads.shape[0])]
    mixed = jnp.stack([pair[0] for pair in outs])
    log_total = jnp.stack([pair[1] for pair in outs])
    attended = stream + (seq_reduce(dot_in(mixed, w_out)) + out_shift)
    normed_two = seq_gather(norm_rows(attended, gain_two, shift_two).astype(BF))
    hidden = dot_in(normed_two, w_up) + up_shift
    activated = jax.nn.gelu(hidden, approximate=False).astype(BF)
    result = attended + (seq_reduce(dot_in(activated, w_down)) + down_shift)
    return (stream, normed_one, heads, log_total, mixed, attended, normed_two, hidden, activated), result


def sum_rows(rows):
    return jnp.sum(rows.astype(F32), axis=(0, 1))


def layer_backward(upstream, weights, state, seq_index, seq_size, fsdp_size):
    gain_one, shift_one, w_qkv, qkv_add, w_out, out_shift, gain_two, shift_two, w_up, up_shift, w_down, down_shift = weights
    stream, normed_one, heads, log_total, mixed, attended, normed_two, hidden, activated = state
    grad_down_local = upstream.astype(BF)
    down_shift_grad = sum_rows(grad_down_local)
    grad_down = seq_gather(grad_down_local)
    w_down_grad = dot_grad(activated, grad_down)
    grad_active = dot_back(grad_down, w_down)
    gelu_pull = jax.vjp(partial(jax.nn.gelu, approximate=False), hidden)[1]
    grad_hidden = gelu_pull(grad_active)[0].astype(BF)
    up_shift_grad = sum_rows(grad_hidden)
    w_up_grad = dot_grad(normed_two, grad_hidden)
    grad_normed_two = seq_reduce(dot_back(grad_hidden, w_up))
    _, pull_two = jax.vjp(norm_rows, attended, gain_two, shift_two)
    grad_attended, gain_two_grad, shift_two_grad = pull_two(grad_normed_two)
    grad_attended = grad_attended + upstream
    grad_out_local = grad_attended.astype(BF)
    out_shift_grad = sum_rows(grad_out_local)
    grad_out = seq_gather(grad_out_local)
    w_out_grad = dot_grad(mixed, grad_out)
    grad_mixed = dot_back(grad_out, w_out).astype(BF)
    grad_projected = jnp.stack(
        [
            attend_backward((heads[clip], log_total[clip], grad_mixed[clip]))
            for clip in range(heads.shape[0])
        ]
    )
    qkv_add_grad = sum_rows(grad_projected)
    w_qkv_grad = dot_grad(normed_one, grad_projected)
    grad_normed_one = seq_reduce(dot_back(grad_projected, w_qkv))
    _, pull_one = jax.vjp(norm_rows, stream, gain_one, shift_one)
    grad_stream, gain_one_grad, shift_one_grad = pull_one(grad_normed_one)
    grad_stream = grad_stream + grad_attended

    out_columns = lax.all_to_all(w_out_grad.astype(BF), "seq", split_axis=1, concat_axis=0, tiled=True)
    local_heads = qkv_add_grad.shape[0] // (3 * HEAD_DIM)
    triple = qkv_add_grad.reshape(local_heads, 3, HEAD_DIM)
    up_parts = put_part(up_shift_grad.reshape(fsdp_size, -1), 1, seq_size, seq_index)
    small = jnp.stack(
        [
            gain_one_grad,
            shift_one_grad,
            put_part(triple[:, 0].reshape(-1), 0, seq_size, seq_index),
            put_part(triple[:, 2].reshape(-1), 0, seq_size, seq_index),
            out_shift_grad,
            gain_two_grad,
            shift_two_grad,
            down_shift_grad,
        ],
        axis=1,
    )
    small = jnp.concatenate([small, up_parts.reshape(D, -1)], axis=1).astype(BF)
    small = jnp.pad(small, ((0, 0), (0, 128 - small.shape[1])))
    big = jnp.concatenate(
        [w_up_grad.astype(BF), w_down_grad.astype(BF), w_qkv_grad.astype(BF), out_columns, small],
        axis=1,
    )
    return grad_stream, big


def reduce_big(big):
    owned = lax.psum_scatter(big, "fsdp", scatter_dimension=0, tiled=True)
    return lax.all_gather(owned, "seq", axis=0, tiled=False)


def unpack_big(gathered, sizes):
    up, down, qkv, out = sizes
    spots = [0, up, up + down, up + down + qkv, up + down + qkv + out]
    rows = gathered.shape[1]
    members = [gathered[:, :, spots[i] : spots[i + 1]].astype(F32) for i in range(4)]
    fsdp_size = D // rows
    seq_size = gathered.shape[0]
    w_up = members[0].reshape(seq_size, rows, fsdp_size, -1).transpose(1, 2, 0, 3).reshape(rows, -1)
    w_down = members[1].reshape(seq_size * rows, -1)
    w_qkv = members[2].transpose(1, 0, 2).reshape(rows, -1)
    w_out = members[3].transpose(1, 0, 2).reshape(rows, -1)
    small = jnp.sum(gathered[:, :, spots[4] :].astype(F32), axis=0)
    return w_qkv, w_out, w_up, w_down, small


def attend_forward(packed):
    frames = packed.shape[0]
    local_heads = packed.shape[1] // (3 * HEAD_DIM)
    parts = packed.reshape(frames, local_heads, 3, HEAD_DIM)
    scores = jnp.einsum(
        "qhd,khd->hqk", parts[:, :, 0], parts[:, :, 1], preferred_element_type=jnp.float32
    ) * HEAD_DIM ** (-0.5)
    peak_score = jnp.max(scores, axis=-1, keepdims=True)
    expanded = jnp.exp(scores - peak_score)
    totals = jnp.sum(expanded, axis=-1, keepdims=True)
    weights = (expanded / totals).astype(jnp.bfloat16)
    mixed = jnp.einsum("hqk,khd->qhd", weights, parts[:, :, 2], preferred_element_type=jnp.float32)
    return (
        mixed.reshape(frames, local_heads * HEAD_DIM).astype(jnp.bfloat16),
        (peak_score + jnp.log(totals))[..., 0],
    )


def attend_backward(inputs):
    packed, log_total, incoming = inputs
    frames = packed.shape[0]
    local_heads = packed.shape[1] // (3 * HEAD_DIM)
    parts = packed.reshape(frames, local_heads, 3, HEAD_DIM)
    queries = parts[:, :, 0]
    keys_local = parts[:, :, 1]
    values_local = parts[:, :, 2]
    scale = HEAD_DIM ** (-0.5)
    scores = (
        jnp.einsum("qhd,khd->hqk", queries, keys_local, preferred_element_type=jnp.float32) * scale
    )
    probs = jnp.exp(scores - log_total[..., None])
    incoming_heads = incoming.reshape(frames, local_heads, HEAD_DIM)
    grad_probs = jnp.einsum(
        "qhd,khd->hqk", incoming_heads, values_local, preferred_element_type=jnp.float32
    )
    grad_values = jnp.einsum(
        "hqk,qhd->khd",
        probs.astype(jnp.bfloat16),
        incoming_heads,
        preferred_element_type=jnp.float32,
    )
    grad_scores = (
        probs * (grad_probs - jnp.sum(probs * grad_probs, axis=-1, keepdims=True))
    ).astype(jnp.bfloat16)
    grad_queries = (
        jnp.einsum("hqk,khd->qhd", grad_scores, keys_local, preferred_element_type=jnp.float32)
        * scale
    )
    grad_keys = (
        jnp.einsum("hqk,qhd->khd", grad_scores, queries, preferred_element_type=jnp.float32) * scale
    )
    stacked = jnp.stack([grad_queries, grad_keys, grad_values], axis=2)
    return stacked.reshape(frames, local_heads * 3 * HEAD_DIM).astype(jnp.bfloat16)


def local(
    frames_in,
    norm1_gain,
    norm1_bias,
    qkv_weight,
    qv_bias,
    out_weight,
    out_bias,
    norm2_gain,
    norm2_bias,
    fc1_weight,
    fc1_bias,
    fc2_weight,
    fc2_bias,
    out_cotangent,
):
    shards = (
        norm1_gain,
        norm1_bias,
        qkv_weight,
        qv_bias,
        out_weight,
        out_bias,
        norm2_gain,
        norm2_bias,
        fc1_weight,
        fc1_bias,
        fc2_weight,
        fc2_bias,
    )
    layer_count = qkv_weight.shape[0]
    fsdp_size = lax.axis_size("fsdp")
    seq_size = lax.axis_size("seq")
    seq_index = lax.axis_index("seq")
    rows = qkv_weight.shape[1]
    part_rows = fc1_bias.shape[1] // seq_size
    hidden_local = fsdp_size * part_rows

    weights = []
    for level in range(layer_count):
        up_part = take_part(fc1_weight[level].reshape(rows, fsdp_size, -1), 2, seq_size, seq_index)
        small = jnp.stack(
            [
                norm1_gain[level],
                norm1_bias[level],
                qv_bias[level, 0],
                qv_bias[level, 1],
                out_bias[level],
                norm2_gain[level],
                norm2_bias[level],
                fc2_bias[level],
            ],
            axis=1,
        )
        small = jnp.concatenate([small, fc1_bias[level].reshape(rows, -1)], axis=1)
        small = jnp.pad(small, ((0, 0), (0, 128 - small.shape[1])))
        lead = jnp.concatenate([small, take_part(qkv_weight[level], 1, seq_size, seq_index)], axis=1)
        lead = lax.all_gather(lead, "fsdp", axis=0, tiled=True)
        packed = jnp.concatenate(
            [
                up_part.reshape(rows, hidden_local),
                take_part(fc2_weight[level], 0, seq_size, seq_index),
                out_weight[level],
            ],
            axis=1,
        )
        packed = lax.all_gather(packed, "fsdp", axis=0, tiled=True)
        w_up = packed[:, :hidden_local]
        w_down = packed[:, hidden_local : hidden_local + D]
        w_qkv = lead[:, 128:]
        w_out = take_part(packed[:, hidden_local + D :], 0, seq_size, seq_index)
        pieces = lead[:, :12].astype(F32)
        vectors = [pieces[:, i] for i in range(8)]
        gain_one, shift_one, query_add, value_add, out_shift, gain_two, shift_two, down_shift = vectors
        up_shift = take_part(pieces[:, 8:].reshape(fsdp_size, -1), 1, seq_size, seq_index)
        up_shift = up_shift.reshape(hidden_local)
        qkv_add = take_part(qkv_shift(jnp.stack([query_add, value_add])), 0, seq_size, seq_index)
        weights.append(
            (gain_one, shift_one, w_qkv, qkv_add, w_out, out_shift, gain_two, shift_two, w_up, up_shift, w_down, down_shift)
        )

    stream = frames_in.astype(F32)
    saved = []
    for level in range(layer_count):
        kept, stream = layer_forward(stream, weights[level])
        saved.append(kept)
    frames_out = stream.astype(BF)
    upstream = out_cotangent.astype(F32)
    reduced = [None] * layer_count
    for level in reversed(range(layer_count)):
        upstream, big = layer_backward(
            upstream, weights[level], saved[level], seq_index, seq_size, fsdp_size
        )
        reduced[level] = unpack_big(
            reduce_big(big), (hidden_local, D, 3 * D // seq_size, D // seq_size)
        )
    qkv_grad, out_grad, up_grad, down_grad, small_grad = [
        jnp.stack([reduced[level][member] for level in range(layer_count)]) for member in range(5)
    ]
    vectors = [small_grad[:, :, i] for i in range(8)]
    up_sum = small_grad[:, :, 8:12].reshape(layer_count, -1)
    return (
        frames_out,
        upstream,
        vectors[0],
        vectors[1],
        qkv_grad,
        jnp.stack([vectors[2], vectors[3]], axis=1),
        out_grad,
        vectors[4],
        vectors[5],
        vectors[6],
        up_grad,
        up_sum,
        down_grad,
        vectors[7],
    )


def solution(mesh):
    in_specs = (
        P("fsdp", "seq", None),
        P(None, "fsdp"),
        P(None, "fsdp"),
        P(None, "fsdp", None),
        P(None, None, "fsdp"),
        P(None, "fsdp", None),
        P(None, "fsdp"),
        P(None, "fsdp"),
        P(None, "fsdp"),
        P(None, "fsdp", None),
        P(None, "fsdp"),
        P(None, "fsdp", None),
        P(None, "fsdp"),
        P("fsdp", "seq", None),
    )
    out_specs = (
        P("fsdp", "seq", None),
        P("fsdp", "seq", None),
        P(None, "fsdp"),
        P(None, "fsdp"),
        P(None, "fsdp", None),
        P(None, None, "fsdp"),
        P(None, "fsdp", None),
        P(None, "fsdp"),
        P(None, "fsdp"),
        P(None, "fsdp"),
        P(None, "fsdp", None),
        P(None, "fsdp"),
        P(None, "fsdp", None),
        P(None, "fsdp"),
    )
    return jax.shard_map(local, mesh=mesh, in_specs=in_specs, out_specs=out_specs, check_vma=False)
```
